32 devices in a mesh: layer: 16 (over z, y, core), rhs: 2 (over x).
Axes of the slice: x: 2, y: 2, z: 4, core: 2. Of those that a mesh axis runs over, the one named last changes fastest.
Arguments:
- diag_block: float32 [32, 384, 384], P('layer'), may hold values from -0.234742767 to 4.6347428, as said below
- coupling: float32 [32, 384, 384], P('layer'), may hold values from -1.76123724 to 1.76123724
- right_side: float32 [32, 384, 256], P('layer', None, 'rhs'), may hold values from -6 to 6
Outputs:
- inverse_out: float32 [32, 384, 384], P('layer')
- rhs_out: float32 [32, 384, 256], P('layer', None, 'rhs')
The draws below stay inside these ranges and needn't reach their ends.
Inputs may be any that keep to these rules, and one draw needn't show every extreme that they name: `diag_block`: each diagonal block is symmetric.
All inputs are finite; a program needn't handle non-finite values.
Results may differ from the reference program's by a relative error of at most 0.00013.
Values sent between devices are 32-bit elements; how exact they have to be, the bound alone decides.
A program may use at most 64 MiB of HBM per device.

```python
import math
import jax
import jax.numpy as jnp
from jax import lax

ORBITALS = 384
NS_ITERS = 3
LEVELS = 3
LAYERS = 32
RHS = 256


def draw_diag_block(key, part):
    key_noise, key_diag = jax.random.split(jax.random.fold_in(key, 11))
    spread = 0.8 / math.sqrt(ORBITALS)
    noise = jnp.clip(jax.random.normal(key_noise, (LAYERS, ORBITALS, ORBITALS), jnp.float32), -4.0, 4.0)
    symmetric = (noise + jnp.swapaxes(noise, 1, 2)) * (spread / math.sqrt(2.0))
    diagonal_vals = jax.random.uniform(key_diag, (LAYERS, ORBITALS), jnp.float32, 3.6, 4.4)
    return symmetric + diagonal_vals[:, :, None] * jnp.eye(ORBITALS, dtype=jnp.float32)[None]


def draw_coupling(key, part):
    key_noise, key_size, key_sign = jax.random.split(jax.random.fold_in(key, 23), 3)
    spread = 0.3 / math.sqrt(ORBITALS)
    noise = jnp.clip(jax.random.normal(key_noise, (LAYERS, ORBITALS, ORBITALS), jnp.float32), -4.0, 4.0)
    magnitude = jax.random.uniform(key_size, (ORBITALS,), jnp.float32, 0.9, 1.7)
    signs = jax.random.rademacher(key_sign, (LAYERS, ORBITALS), jnp.float32)
    onsite = signs * magnitude[None, :]
    return noise * spread + onsite[:, :, None] * jnp.eye(ORBITALS, dtype=jnp.float32)[None]


def levels(rng, shape, pieces, low, high):
    loudness = 1.0
    for axis_at, blocks in pieces:
        heights = jax.random.uniform(jax.random.fold_in(jax.random.fold_in(rng, 6), axis_at), (blocks,), jnp.float32, low / len(pieces), high / len(pieces))
        loudness = loudness * jnp.repeat(jnp.exp(heights), shape[axis_at] // blocks).reshape((-1,) + (1,) * (len(shape) - 1 - axis_at))
    return loudness


def centred(rng, dims, width, most, cuts=(), kind=jnp.bfloat16):
    entries = width * jax.random.normal(rng, dims, jnp.float32)
    if cuts:
        entries = entries * levels(rng, dims, cuts, -0.22, 0.18)
    return jnp.clip(entries, -most, most).astype(kind)


def setup_inputs(seed: int = 0) -> dict:
    key_of = jax.random.split(jax.random.key(seed), 4)
    return {
        "diag_block": draw_diag_block(jax.random.fold_in(key_of[3], 71), 0),
        "coupling": draw_coupling(jax.random.fold_in(key_of[3], 71), 0),
        "right_side": centred(key_of[2], (LAYERS, ORBITALS, RHS), 1.0, 6.0, ((0, 16), (2, 2)), jnp.float32),
    }


def invert(blocks):
    trace_vals = jnp.trace(blocks, axis1=1, axis2=2)
    identity = jnp.eye(ORBITALS, dtype=blocks.dtype)
    approx = identity[None] * (ORBITALS / trace_vals)[:, None, None]
    for sweep in range(NS_ITERS):
        product = jnp.einsum('bij,bjk->bik', blocks, approx, precision=lax.Precision.HIGHEST)
        approx = 2.0 * approx - jnp.einsum('bij,bjk->bik', approx, product, precision=lax.Precision.HIGHEST)
    return approx


def reference(diag_block, coupling, right_side):
    diag_now, coupling_now, rhs_now = diag_block, coupling, right_side
    inverse_out = jnp.zeros_like(diag_block)
    rhs_out = jnp.zeros_like(right_side)
    for level_num in range(LEVELS):
        stride = 2 ** level_num
        removed_idx = jnp.arange(stride - 1, LAYERS, 2 * stride)
        kept_idx = jnp.arange(2 * stride - 1, LAYERS, 2 * stride)
        approx = invert(diag_now[removed_idx])
        u_left = jnp.roll(coupling_now[kept_idx], 1, axis=0)
        u_self = coupling_now[removed_idx]
        r_self = rhs_now[removed_idx]
        stacked = jnp.concatenate([jnp.swapaxes(u_left, 1, 2), u_self, r_self], axis=2)
        solved = jnp.einsum('bij,bjk->bik', approx, stacked, precision=lax.Precision.HIGHEST)
        left_part = jnp.einsum('bij,bjk->bik', u_left, solved, precision=lax.Precision.HIGHEST)
        right_part = jnp.einsum('bji,bjk->bik', u_self, solved[:, :, ORBITALS:], precision=lax.Precision.HIGHEST)
        inverse_out = inverse_out.at[removed_idx].set(approx)
        rhs_out = rhs_out.at[removed_idx].set(r_self)
        from_right = jnp.roll(left_part, -1, axis=0)
        diag_now = diag_now.at[kept_idx].set(diag_now[kept_idx] - from_right[:, :, :ORBITALS] - right_part[:, :, :ORBITALS])
        coupling_now = coupling_now.at[kept_idx].set(-from_right[:, :, ORBITALS:2 * ORBITALS])
        rhs_now = rhs_now.at[kept_idx].set(rhs_now[kept_idx] - from_right[:, :, 2 * ORBITALS:] - right_part[:, :, ORBITALS:])
    final_idx = jnp.arange(2 ** LEVELS - 1, LAYERS, 2 ** LEVELS)
    inverse_out = inverse_out.at[final_idx].set(invert(diag_now[final_idx]))
    rhs_out = rhs_out.at[final_idx].set(rhs_now[final_idx])
    return (inverse_out, rhs_out)
```

```python
import jax
import jax.numpy as jnp
from jax import lax
from jax.sharding import PartitionSpec as P

LEVELS = 3


def passed_along(block, axis, distance):
    devices = range(lax.axis_size(axis))
    route = [((i - distance) % len(devices), i) for i in devices]
    return lax.ppermute(block, axis, route)


def matmul(first, second):
    return jnp.dot(
        first, second, precision=lax.Precision.HIGH, preferred_element_type=jnp.float32
    )


def invert(block_now):
    orbitals = block_now.shape[0]
    identity = jnp.eye(orbitals, dtype=jnp.float32)
    scale = orbitals / jnp.trace(block_now)
    err = identity - scale * block_now
    square = matmul(err, err)
    approx = scale * (identity + err)
    approx = approx + matmul(approx, square)
    return approx + matmul(approx, matmul(square, square))


def prepare(operands):
    approx, u_self, r_self = operands
    solved = matmul(approx, jnp.concatenate([u_self, r_self], axis=1))
    return (solved, matmul(u_self.T, solved))


def prepare_skip(operands):
    approx, u_self, r_self = operands
    width = u_self.shape[1] + r_self.shape[1]
    empty = jnp.zeros((approx.shape[0], width), jnp.float32)
    return (empty, empty)


def eliminate(operands):
    diag_now, u_self, r_self = operands
    approx = invert(diag_now)
    solved, right_part = prepare((approx, u_self, r_self))
    return (approx, solved, right_part)


def eliminate_skip(operands):
    diag_now, u_self, r_self = operands
    solved, right_part = prepare_skip((diag_now, u_self, r_self))
    return (jnp.zeros_like(diag_now), solved, right_part)


def complete(operands):
    u_left, approx, solved = operands
    first = matmul(approx, u_left.T)
    return matmul(u_left, jnp.concatenate([first, solved], axis=1))


def complete_skip(operands):
    u_left, approx, solved = operands
    return jnp.zeros((u_left.shape[0], u_left.shape[1] + solved.shape[1]), jnp.float32)


def lift(first, second, stride):
    return passed_along((first, second), "layer", stride)


def send_down(left_part, stride, blocks):
    orbitals = left_part.shape[0]
    columns = blocks * orbitals
    head = left_part[:, :columns]
    tail = left_part[:, 2 * orbitals :]
    head_in, tail_in = passed_along((head, tail), "layer", -stride)
    return (head_in, tail_in)


def body(diag_block, coupling, right_side):
    orbitals = diag_block.shape[1]
    position = lax.axis_index("layer")
    low_diag, high_diag = (diag_block[0], diag_block[1])
    low_coup, high_coup = (coupling[0], coupling[1])
    low_rhs, high_rhs = (right_side[0], right_side[1])
    low_inverse = invert(low_diag)
    solved, right_part = prepare((low_inverse, low_coup, low_rhs))
    first_in, second_in = lift(high_coup, jnp.zeros_like(high_rhs), 1)
    left_part = complete((first_in, low_inverse, solved))
    head_in, tail_in = send_down(left_part, 1, 2)
    high_diag = high_diag - head_in[:, :orbitals] - right_part[:, :orbitals]
    high_coup = -head_in[:, orbitals : 2 * orbitals]
    high_rhs = high_rhs - tail_in - right_part[:, orbitals:]
    high_inverse = jnp.zeros_like(high_diag)
    high_record = jnp.zeros_like(high_rhs)
    for level_num in range(1, LEVELS):
        stride = 2 ** (level_num - 1)
        phase = (position + 1) % (2 * stride)
        removed = phase == stride
        survive = phase == 0
        approx, solved, right_part = lax.cond(
            removed, eliminate, eliminate_skip, (high_diag, high_coup, high_rhs)
        )
        first = jnp.where(removed, right_part[:, :orbitals], high_coup)
        second = jnp.where(removed, right_part[:, orbitals:], jnp.zeros_like(high_rhs))
        first_in, second_in = lift(first, second, stride)
        left_part = lax.cond(removed, complete, complete_skip, (first_in, approx, solved))
        blocks = 2 if level_num < LEVELS - 1 else 1
        head_in, tail_in = send_down(left_part, stride, blocks)
        high_inverse = jnp.where(removed, approx, high_inverse)
        high_record = jnp.where(removed, high_rhs, high_record)
        high_diag = jnp.where(survive, high_diag - head_in[:, :orbitals] - first_in, high_diag)
        high_rhs = jnp.where(survive, high_rhs - tail_in - second_in, high_rhs)
        if blocks == 2:
            high_coup = jnp.where(survive, -head_in[:, orbitals : 2 * orbitals], high_coup)
    final_keep = (position + 1) % 2 ** (LEVELS - 1) == 0
    final_inverse = lax.cond(final_keep, invert, jnp.zeros_like, high_diag)
    high_inverse = jnp.where(final_keep, final_inverse, high_inverse)
    high_record = jnp.where(final_keep, high_rhs, high_record)
    inverse_out = jnp.stack([low_inverse, high_inverse], axis=0)
    rhs_out = jnp.stack([low_rhs, high_record], axis=0)
    return (inverse_out, rhs_out)


def solution(mesh):
    return jax.shard_map(
        body,
        mesh=mesh,
        in_specs=(P("layer", None, None), P("layer", None, None), P("layer", None, "rhs")),
        out_specs=(P("layer", None, None), P("layer", None, "rhs")),
        check_vma=False,
    )
```

```python
import functools

import jax
import jax.numpy as jnp
from jax import lax
from jax.experimental import pallas as pl
from jax.experimental.pallas import tpu as pltpu
from jax.sharding import PartitionSpec as P

LEVELS = 3
TILE = 128


def split(value):
    high = value.astype(jnp.bfloat16)
    return high, (value - high.astype(jnp.float32)).astype(jnp.bfloat16)


def matmul(first, second, transposed=False):
    dims = (((1,), (1 if transposed else 0,)), ((), ()))

    def one(a, b):
        return lax.dot_general(a, b, dims, preferred_element_type=jnp.float32)

    return one(first[0], second[0]) + (one(first[0], second[1]) + one(first[1], second[0]))


def invert(block):
    orbitals = block.shape[0]
    rows = lax.broadcasted_iota(jnp.int32, (orbitals, orbitals), 0)
    columns = lax.broadcasted_iota(jnp.int32, (orbitals, orbitals), 1)
    on_diag = rows == columns
    trace = jnp.sum(jnp.where(on_diag, block, 0.0), axis=(0, 1), keepdims=True)
    scale = orbitals / trace
    identity = jnp.where(on_diag, 1.0, 0.0)
    err = identity - scale * block
    err_parts = split(err)
    square = matmul(err_parts, err_parts)
    square_parts = split(square)
    rest = err + (square + matmul(err_parts, square_parts))
    fourth = matmul(square_parts, square_parts)
    return scale * (identity + (rest + (fourth + matmul(split(rest), split(fourth)))))


def kernel(size, d_ref, u_ref, r_ref, inv_ref, rec_ref, d_now, u_now, x_in, u_in, r_in,
           q_out, q_in, s_out, s_in, send_sem, recv_sem):
    me = lax.axis_index("layer")
    orbitals = d_ref.shape[1]
    tiles = orbitals // TILE

    def at(distance):
        return {"layer": lax.rem(me + distance + size, size)}

    strides = [2 ** level for level in range(LEVELS - 1)]
    partners = [sign * stride for stride in strides for sign in (1, -1)]
    barrier = pltpu.get_barrier_semaphore()
    for distance in partners:
        pl.semaphore_signal(barrier, inc=1, device_id=at(distance), device_id_type=pl.DeviceIdType.MESH)
    pl.semaphore_wait(barrier, len(partners))

    def remote(src, dst, level, slot, distance):
        return pltpu.make_async_remote_copy(
            src_ref=src, dst_ref=dst, send_sem=send_sem.at[level, slot],
            recv_sem=recv_sem.at[level, slot], device_id=at(distance),
            device_id_type=pl.DeviceIdType.MESH,
        )

    def triangle(src, dst, level, slot, distance):
        copies = []
        for i in range(tiles):
            part = (pl.ds(i * TILE, TILE), pl.ds(i * TILE, orbitals - i * TILE))
            copies.append(remote(src.at[part], dst.at[part], level, slot + i, distance))
        return copies

    def mirror(ref):
        for i in range(tiles):
            for j in range(i + 1, tiles):
                low, high = pl.ds(i * TILE, TILE), pl.ds(j * TILE, TILE)
                ref[high, low] = ref[low, high].T

    def operands(level, stride):
        src_u, src_r = (u_ref.at[0], r_ref.at[0]) if level == 0 else (u_now, rec_ref.at[1])
        copies = [remote(src_r, r_in.at[level], level, 1, -stride)]
        if level < LEVELS - 1:
            copies.append(remote(src_u, u_in.at[level], level, 0, -stride))
        return copies

    def inverse_copies(level, stride):
        return triangle(inv_ref.at[min(level, 1)], x_in.at[level], level, 2, -stride)

    def right_copies(level, stride):
        return triangle(q_out, q_in.at[level - 1], level, 2 + tiles, stride) + [
            remote(s_out, s_in.at[level - 1], level, 2 + 2 * tiles, stride)
        ]

    def right_part(approx, u_self, r_self):
        parts = split(approx)
        turned = split(u_self.T)
        return (
            matmul(turned, split(matmul(parts, split(u_self)))),
            matmul(turned, split(matmul(parts, split(r_self)))),
        )

    def complete(level, stride, u_left):
        for copy in operands(level, stride) + inverse_copies(level, stride):
            copy.wait_recv()
        mirror(x_in.at[level])
        left = split(u_left[...])
        through = split(matmul(left, split(x_in[level])))
        d_now[...] -= matmul(through, left, transposed=True)
        rec_ref[1] -= matmul(through, split(r_in[level]))
        if level < LEVELS - 1:
            u_now[...] = -matmul(through, split(u_in[level]))

    first_level = operands(0, 1)
    for copy in first_level:
        copy.start()
    rec_ref[0] = r_ref[0]
    inv_ref[0] = invert(d_ref[0])
    for copy in inverse_copies(0, 1):
        copy.start()
    q_diag, q_rhs = right_part(inv_ref[0], u_ref[0], r_ref[0])
    d_now[...] = d_ref[1] - q_diag
    rec_ref[1] = r_ref[1] - q_rhs
    complete(0, 1, u_ref.at[1])

    for level in range(1, LEVELS):
        stride = 2 ** (level - 1)
        phase = lax.rem(me + 1, 2 * stride)

        @pl.when(phase == stride)
        def _():
            early = operands(level, stride)
            for copy in early:
                copy.start()
            inv_ref[1] = invert(d_now[...])
            middle = inverse_copies(level, stride)
            for copy in middle:
                copy.start()
            q_diag, q_rhs = right_part(inv_ref[1], u_now[...], rec_ref[1])
            q_out[...] = q_diag
            s_out[...] = q_rhs
            late = right_copies(level, stride)
            for copy in late:
                copy.start()
            for copy in early + middle + late:
                copy.wait_send()

        @pl.when(phase == 0)
        def _():
            for copy in right_copies(level, stride):
                copy.wait_recv()
            mirror(q_in.at[level - 1])
            d_now[...] -= q_in[level - 1]
            rec_ref[1] -= s_in[level - 1]
            complete(level, stride, u_now)

    @pl.when(lax.rem(me + 1, 2 ** (LEVELS - 1)) == 0)
    def _():
        inv_ref[1] = invert(d_now[...])

    for copy in operands(0, 1) + inverse_copies(0, 1):
        copy.wait_send()


def body(diag_block, coupling, right_side):
    orbitals, columns = right_side.shape[1:]
    tiles = orbitals // TILE
    square, side = (orbitals, orbitals), (orbitals, columns)
    slots = 3 + 2 * tiles
    vmem = pl.BlockSpec(memory_space=pltpu.VMEM)
    return pl.pallas_call(
        functools.partial(kernel, lax.axis_size("layer")),
        out_shape=(
            jax.ShapeDtypeStruct(diag_block.shape, jnp.float32),
            jax.ShapeDtypeStruct(right_side.shape, jnp.float32),
        ),
        in_specs=[vmem] * 3,
        out_specs=(vmem, vmem),
        scratch_shapes=[
            pltpu.VMEM(square, jnp.float32),
            pltpu.VMEM(square, jnp.float32),
            pltpu.VMEM((LEVELS,) + square, jnp.float32),
            pltpu.VMEM((LEVELS - 1,) + square, jnp.float32),
            pltpu.VMEM((LEVELS,) + side, jnp.float32),
            pltpu.VMEM(square, jnp.float32),
            pltpu.VMEM((LEVELS - 1,) + square, jnp.float32),
            pltpu.VMEM(side, jnp.float32),
            pltpu.VMEM((LEVELS - 1,) + side, jnp.float32),
            pltpu.SemaphoreType.DMA((LEVELS, slots)),
            pltpu.SemaphoreType.DMA((LEVELS, slots)),
        ],
        compiler_params=pltpu.CompilerParams(
            collective_id=0, has_side_effects=True, vmem_limit_bytes=48 * 2 ** 20
        ),
    )(diag_block, coupling, right_side)


def solution(mesh):
    return jax.shard_map(
        body,
        mesh=mesh,
        in_specs=(P("layer", None, None), P("layer", None, None), P("layer", None, "rhs")),
        out_specs=(P("layer", None, None), P("layer", None, "rhs")),
        check_vma=False,
    )
```

```python
import functools

import jax
import jax.numpy as jnp
from jax import lax
from jax.experimental import pallas as pl
from jax.experimental.pallas import tpu as pltpu
from jax.sharding import PartitionSpec as P

LEVELS = 3
TILE = 128


def split(value):
    high = value.astype(jnp.bfloat16)
    return high, (value - high.astype(jnp.float32)).astype(jnp.bfloat16)


def matmul(first, second, transposed=False):
    dims = (((1,), (1 if transposed else 0,)), ((), ()))

    def one(a, b):
        return lax.dot_general(a, b, dims, preferred_element_type=jnp.float32)

    return one(first[0], second[0]) + (one(first[0], second[1]) + one(first[1], second[0]))


def invert(block):
    orbitals = block.shape[0]
    rows = lax.broadcasted_iota(jnp.int32, (orbitals, orbitals), 0)
    columns = lax.broadcasted_iota(jnp.int32, (orbitals, orbitals), 1)
    on_diag = rows == columns
    trace = jnp.sum(jnp.where(on_diag, block, 0.0), axis=(0, 1), keepdims=True)
    scale = orbitals / trace
    identity = jnp.where(on_diag, 1.0, 0.0)
    err = identity - scale * block
    err_parts = split(err)
    square = matmul(err_parts, err_parts)
    square_parts = split(square)
    rest = err + (square + matmul(err_parts, square_parts))
    fourth = matmul(square_parts, square_parts)
    return scale * (identity + (rest + (fourth + matmul(split(rest), split(fourth)))))


def kernel(size, ways, d_ref, u_ref, r_ref, inv_ref, rec_ref, d_now, u_now, x_in, u_in, r_in,
           q_out, q_in, s_out, s_in, send_sem, recv_sem, pass_sem):
    me = lax.axis_index("layer")
    side = lax.axis_index("rhs")
    orbitals = d_ref.shape[1]
    tiles = orbitals // TILE

    def at(distance):
        return {"layer": lax.rem(me + distance + size, size)}

    def across(hop):
        return {"rhs": lax.rem(side + hop, ways)}

    strides = [2 ** level for level in range(LEVELS - 1)]
    partners = [sign * stride for stride in strides for sign in (1, -1)]
    barrier = pltpu.get_barrier_semaphore()
    for distance in partners:
        pl.semaphore_signal(barrier, inc=1, device_id=at(distance), device_id_type=pl.DeviceIdType.MESH)
    for hop in range(1, ways):
        pl.semaphore_signal(barrier, inc=1, device_id=across(hop), device_id_type=pl.DeviceIdType.MESH)
    pl.semaphore_wait(barrier, len(partners) + ways - 1)

    def remote(src, dst, level, slot, distance):
        return pltpu.make_async_remote_copy(
            src_ref=src, dst_ref=dst, send_sem=send_sem.at[level, slot],
            recv_sem=recv_sem.at[level, slot], device_id=at(distance),
            device_id_type=pl.DeviceIdType.MESH,
        )

    def triangle(src, dst, slot):
        pieces = []
        for i in range(tiles):
            part = (pl.ds(i * TILE, TILE), pl.ds(i * TILE, orbitals - i * TILE))
            pieces.append((src.at[part], dst.at[part], slot + i, min(i, ways - 1)))
        return pieces

    def bands(src, dst, slot):
        rows = orbitals // ways
        parts = [pl.ds(i * rows, rows) for i in range(ways)]
        return [(src.at[part], dst.at[part], slot + i, i) for i, part in enumerate(parts)]

    def u_pieces(level):
        return bands(u_ref.at[0] if level == 0 else u_now, u_in.at[level], 2 + 2 * tiles)

    def x_pieces(level):
        return triangle(inv_ref.at[min(level, 1)], x_in.at[level], 1)

    def q_pieces(level):
        return triangle(q_out, q_in.at[level - 1], 1 + tiles)

    def r_copy(level, stride):
        src = r_ref.at[0] if level == 0 else rec_ref.at[1]
        return remote(src, r_in.at[level], level, 0, -stride)

    def s_copy(level, stride):
        return remote(s_out, s_in.at[level - 1], level, 1 + 2 * tiles, stride)

    def mine(owner, whole):
        return jnp.logical_or(side == owner, whole)

    def give(pieces, level, distance, whole):
        for src, dst, slot, owner in pieces:
            @pl.when(mine(owner, whole))
            def _():
                remote(src, dst, level, slot, distance).start()

    def given(pieces, level, distance, whole):
        for src, dst, slot, owner in pieces:
            @pl.when(mine(owner, whole))
            def _():
                remote(src, dst, level, slot, distance).wait_send()

    def passing(dst, level, slot, hop):
        return pltpu.make_async_remote_copy(
            src_ref=dst, dst_ref=dst, send_sem=pass_sem.at[level, slot, hop - 1],
            recv_sem=recv_sem.at[level, slot], device_id=across(hop),
            device_id_type=pl.DeviceIdType.MESH,
        )

    def relays(owner, whole):
        return jnp.logical_and(side == owner, jnp.logical_not(whole))

    def relay(pieces, level, whole):
        for src, dst, slot, owner in pieces:
            @pl.when(relays(owner, whole))
            def _():
                remote(src, dst, level, slot, 1).wait_recv()
                for hop in range(1, ways):
                    passing(dst, level, slot, hop).start()

    def take(pieces, level, whole):
        for src, dst, slot, owner in pieces:
            @pl.when(jnp.logical_not(relays(owner, whole)))
            def _():
                remote(src, dst, level, slot, 1).wait_recv()

    def relayed(pieces, level, whole):
        for src, dst, slot, owner in pieces:
            @pl.when(relays(owner, whole))
            def _():
                for hop in range(1, ways):
                    passing(dst, level, slot, hop).wait_send()

    def mirror(ref):
        for i in range(tiles):
            for j in range(i + 1, tiles):
                low, high = pl.ds(i * TILE, TILE), pl.ds(j * TILE, TILE)
                ref[high, low] = ref[low, high].T

    def right_part(approx, u_self, r_self):
        parts = split(approx)
        turned = split(u_self.T)
        return (
            matmul(turned, split(matmul(parts, split(u_self)))),
            matmul(turned, split(matmul(parts, split(r_self)))),
        )

    def complete(level, stride, u_left, whole):
        last = level == LEVELS - 1
        if not last and level > 0:
            relay(u_pieces(level), level, whole)
        relay(x_pieces(level), level, whole)
        r_copy(level, stride).wait_recv()
        if not last:
            take(u_pieces(level), level, whole)
        take(x_pieces(level), level, whole)
        mirror(x_in.at[level])
        left = split(u_left[...])
        through = split(matmul(left, split(x_in[level])))
        d_now[...] -= matmul(through, left, transposed=True)
        rec_ref[1] -= matmul(through, split(r_in[level]))
        if level < LEVELS - 1:
            u_now[...] = -matmul(through, split(u_in[level]))

    whole_out = lax.rem(me, 2) == 1
    whole_in = lax.rem(me, 2) == 0
    r_copy(0, 1).start()
    give(u_pieces(0), 0, -1, whole_out)
    rec_ref[0] = r_ref[0]
    inv_ref[0] = invert(d_ref[0])
    give(x_pieces(0), 0, -1, whole_out)
    relay(u_pieces(0), 0, whole_in)
    q_diag, q_rhs = right_part(inv_ref[0], u_ref[0], r_ref[0])
    d_now[...] = d_ref[1] - q_diag
    rec_ref[1] = r_ref[1] - q_rhs
    complete(0, 1, u_ref.at[1], whole_in)

    for level in range(1, LEVELS):
        stride = 2 ** (level - 1)
        phase = lax.rem(me + 1, 2 * stride)
        last = level == LEVELS - 1
        whole_q = lax.rem(me, 1) == (0 if level == 1 else 1)
        split_l = lax.rem(me, 1) == 1

        @pl.when(phase == stride)
        def _():
            r_copy(level, stride).start()
            if not last:
                give(u_pieces(level), level, -stride, split_l)
            inv_ref[1] = invert(d_now[...])
            give(x_pieces(level), level, -stride, split_l)
            q_diag, q_rhs = right_part(inv_ref[1], u_now[...], rec_ref[1])
            q_out[...] = q_diag
            s_out[...] = q_rhs
            give(q_pieces(level), level, stride, whole_q)
            s_copy(level, stride).start()
            r_copy(level, stride).wait_send()
            if not last:
                given(u_pieces(level), level, -stride, split_l)
            given(x_pieces(level), level, -stride, split_l)
            given(q_pieces(level), level, stride, whole_q)
            s_copy(level, stride).wait_send()

        @pl.when(phase == 0)
        def _():
            complete(level, stride, u_now, split_l)
            relay(q_pieces(level), level, whole_q)
            take(q_pieces(level), level, whole_q)
            s_copy(level, stride).wait_recv()
            mirror(q_in.at[level - 1])
            d_now[...] -= q_in[level - 1]
            rec_ref[1] -= s_in[level - 1]
            if not last:
                relayed(u_pieces(level), level, split_l)
            relayed(x_pieces(level), level, split_l)
            relayed(q_pieces(level), level, whole_q)

    @pl.when(lax.rem(me + 1, 2 ** (LEVELS - 1)) == 0)
    def _():
        inv_ref[1] = invert(d_now[...])

    r_copy(0, 1).wait_send()
    given(u_pieces(0), 0, -1, whole_out)
    given(x_pieces(0), 0, -1, whole_out)
    relayed(u_pieces(0), 0, whole_in)
    relayed(x_pieces(0), 0, whole_in)


def body(diag_block, coupling, right_side):
    orbitals, columns = right_side.shape[1:]
    tiles = orbitals // TILE
    square, side = (orbitals, orbitals), (orbitals, columns)
    ways = lax.axis_size("rhs")
    slots = 2 + 2 * tiles + ways
    vmem = pl.BlockSpec(memory_space=pltpu.VMEM)
    return pl.pallas_call(
        functools.partial(kernel, lax.axis_size("layer"), ways),
        out_shape=(
            jax.ShapeDtypeStruct(diag_block.shape, jnp.float32),
            jax.ShapeDtypeStruct(right_side.shape, jnp.float32),
        ),
        in_specs=[vmem] * 3,
        out_specs=(vmem, vmem),
        scratch_shapes=[
            pltpu.VMEM(square, jnp.float32),
            pltpu.VMEM(square, jnp.float32),
            pltpu.VMEM((LEVELS,) + square, jnp.float32),
            pltpu.VMEM((LEVELS - 1,) + square, jnp.float32),
            pltpu.VMEM((LEVELS,) + side, jnp.float32),
            pltpu.VMEM(square, jnp.float32),
            pltpu.VMEM((LEVELS - 1,) + square, jnp.float32),
            pltpu.VMEM(side, jnp.float32),
            pltpu.VMEM((LEVELS - 1,) + side, jnp.float32),
            pltpu.SemaphoreType.DMA((LEVELS, slots)),
            pltpu.SemaphoreType.DMA((LEVELS, slots)),
            pltpu.SemaphoreType.DMA((LEVELS, slots, max(1, ways - 1))),
        ],
        compiler_params=pltpu.CompilerParams(
            collective_id=0, has_side_effects=True, vmem_limit_bytes=48 * 2 ** 20
        ),
    )(diag_block, coupling, right_side)


def solution(mesh):
    return jax.shard_map(
        body,
        mesh=mesh,
        in_specs=(P("layer", None, None), P("layer", None, None), P("layer", None, "rhs")),
        out_specs=(P("layer", None, None), P("layer", None, "rhs")),
        check_vma=False,
    )
```

```python
import functools

import jax
import jax.numpy as jnp
from jax import lax
from jax.experimental import pallas as pl
from jax.experimental.pallas import tpu as pltpu
from jax.sharding import PartitionSpec as P

LEVELS = 3
TILE = 128


def split(value):
    high = value.astype(jnp.bfloat16)
    return high, (value - high.astype(jnp.float32)).astype(jnp.bfloat16)


def matmul(first, second, transposed=False):
    dims = (((1,), (1 if transposed else 0,)), ((), ()))

    def one(a, b):
        return lax.dot_general(a, b, dims, preferred_element_type=jnp.float32)

    return one(first[0], second[0]) + (one(first[0], second[1]) + one(first[1], second[0]))


def beside(first, second):
    return tuple(jnp.concatenate(pair, axis=1) for pair in zip(first, second))


def invert(block):
    orbitals = block.shape[0]
    rows = lax.broadcasted_iota(jnp.int32, (orbitals, orbitals), 0)
    columns = lax.broadcasted_iota(jnp.int32, (orbitals, orbitals), 1)
    on_diag = rows == columns
    trace = jnp.sum(jnp.where(on_diag, block, 0.0), axis=(0, 1), keepdims=True)
    scale = orbitals / trace
    identity = jnp.where(on_diag, 1.0, 0.0)
    err = identity - scale * block
    err_parts = split(err)
    square = matmul(err_parts, err_parts)
    square_parts = split(square)
    both = matmul(square_parts, beside(err_parts, square_parts))
    rest = err + (square + both[:, :orbitals])
    fourth = both[:, orbitals:]
    return scale * (identity + (rest + (fourth + matmul(split(rest), split(fourth)))))


def kernel(size, ways, d_ref, u_ref, r_ref, inv_ref, rec_ref, d_now, u_now, x_in, u_in, r_in,
           q_out, q_in, s_out, s_in, send_sem, recv_sem, pass_sem):
    me = lax.axis_index("layer")
    side = lax.axis_index("rhs")
    orbitals = d_ref.shape[1]
    tiles = orbitals // TILE

    def at(distance):
        return {"layer": lax.rem(me + distance + size, size)}

    def across(hop):
        return {"rhs": lax.rem(side + hop, ways)}

    strides = [2 ** level for level in range(LEVELS - 1)]
    partners = [sign * stride for stride in strides for sign in (1, -1)]
    barrier = pltpu.get_barrier_semaphore()
    for distance in partners:
        pl.semaphore_signal(barrier, inc=1, device_id=at(distance), device_id_type=pl.DeviceIdType.MESH)
    for hop in range(1, ways):
        pl.semaphore_signal(barrier, inc=1, device_id=across(hop), device_id_type=pl.DeviceIdType.MESH)
    pl.semaphore_wait(barrier, len(partners) + ways - 1)

    def remote(src, dst, level, slot, distance):
        return pltpu.make_async_remote_copy(
            src_ref=src, dst_ref=dst, send_sem=send_sem.at[level, slot],
            recv_sem=recv_sem.at[level, slot], device_id=at(distance),
            device_id_type=pl.DeviceIdType.MESH,
        )

    def triangle(src, dst, slot):
        pieces = []
        for i in range(tiles):
            part = (pl.ds(i * TILE, TILE), pl.ds(i * TILE, orbitals - i * TILE))
            pieces.append((src.at[part], dst.at[part], slot + i, min(i, ways - 1)))
        return pieces

    def bands(src, dst, slot):
        rows = orbitals // ways
        parts = [pl.ds(i * rows, rows) for i in range(ways)]
        return [(src.at[part], dst.at[part], slot + i, i) for i, part in enumerate(parts)]

    def u_pieces(level):
        return bands(u_ref.at[0] if level == 0 else u_now, u_in.at[level], 2 + 2 * tiles)

    def x_pieces(level):
        return triangle(inv_ref.at[min(level, 1)], x_in.at[level], 1)

    def q_pieces(level):
        return triangle(q_out, q_in.at[level - 1], 1 + tiles)

    def r_copy(level, stride):
        src = r_ref.at[0] if level == 0 else rec_ref.at[1]
        return remote(src, r_in.at[level], level, 0, -stride)

    def s_copy(level, stride):
        return remote(s_out, s_in.at[level - 1], level, 1 + 2 * tiles, stride)

    def mine(owner, whole):
        return jnp.logical_or(side == owner, whole)

    def give(pieces, level, distance, whole):
        for src, dst, slot, owner in pieces:
            @pl.when(mine(owner, whole))
            def _():
                remote(src, dst, level, slot, distance).start()

    def given(pieces, level, distance, whole):
        for src, dst, slot, owner in pieces:
            @pl.when(mine(owner, whole))
            def _():
                remote(src, dst, level, slot, distance).wait_send()

    def passing(dst, level, slot, hop):
        return pltpu.make_async_remote_copy(
            src_ref=dst, dst_ref=dst, send_sem=pass_sem.at[level, slot, hop - 1],
            recv_sem=recv_sem.at[level, slot], device_id=across(hop),
            device_id_type=pl.DeviceIdType.MESH,
        )

    def relays(owner, whole):
        return jnp.logical_and(side == owner, jnp.logical_not(whole))

    def relay(pieces, level, whole):
        for src, dst, slot, owner in pieces:
            @pl.when(relays(owner, whole))
            def _():
                remote(src, dst, level, slot, 1).wait_recv()
                for hop in range(1, ways):
                    passing(dst, level, slot, hop).start()

    def take(pieces, level, whole):
        for src, dst, slot, owner in pieces:
            @pl.when(jnp.logical_not(relays(owner, whole)))
            def _():
                remote(src, dst, level, slot, 1).wait_recv()

    def relayed(pieces, level, whole):
        for src, dst, slot, owner in pieces:
            @pl.when(relays(owner, whole))
            def _():
                for hop in range(1, ways):
                    passing(dst, level, slot, hop).wait_send()

    def mirror(ref):
        for i in range(tiles):
            for j in range(i + 1, tiles):
                low, high = pl.ds(i * TILE, TILE), pl.ds(j * TILE, TILE)
                ref[high, low] = ref[low, high].T

    def right_part(approx, u_self, r_self):
        parts = split(approx)
        turned = split(u_self.T)
        solved = matmul(parts, beside(split(u_self), split(r_self)))
        reduced = matmul(turned, split(solved))
        return reduced[:, :orbitals], reduced[:, orbitals:]

    def complete(level, stride, u_left, whole):
        last = level == LEVELS - 1
        if not last and level > 0:
            relay(u_pieces(level), level, whole)
        relay(x_pieces(level), level, whole)
        r_copy(level, stride).wait_recv()
        if not last:
            take(u_pieces(level), level, whole)
        take(x_pieces(level), level, whole)
        mirror(x_in.at[level])
        left = split(u_left[...])
        through = split(matmul(left, split(x_in[level])))
        d_now[...] -= matmul(through, left, transposed=True)
        if last:
            rec_ref[1] -= matmul(through, split(r_in[level]))
        else:
            left_part = matmul(through, beside(split(u_in[level]), split(r_in[level])))
            u_now[...] = -left_part[:, :orbitals]
            rec_ref[1] -= left_part[:, orbitals:]

    whole_out = lax.rem(me, 2) == 1
    whole_in = lax.rem(me, 2) == 0
    r_copy(0, 1).start()
    give(u_pieces(0), 0, -1, whole_out)
    rec_ref[0] = r_ref[0]
    inv_ref[0] = invert(d_ref[0])
    give(x_pieces(0), 0, -1, whole_out)
    relay(u_pieces(0), 0, whole_in)
    q_diag, q_rhs = right_part(inv_ref[0], u_ref[0], r_ref[0])
    d_now[...] = d_ref[1] - q_diag
    rec_ref[1] = r_ref[1] - q_rhs
    complete(0, 1, u_ref.at[1], whole_in)

    for level in range(1, LEVELS):
        stride = 2 ** (level - 1)
        phase = lax.rem(me + 1, 2 * stride)
        last = level == LEVELS - 1
        whole_q = lax.rem(me, 1) == (0 if level == 1 else 1)
        split_l = lax.rem(me, 1) == 1

        @pl.when(phase == stride)
        def _():
            r_copy(level, stride).start()
            if not last:
                give(u_pieces(level), level, -stride, split_l)
            inv_ref[1] = invert(d_now[...])
            give(x_pieces(level), level, -stride, split_l)
            q_diag, q_rhs = right_part(inv_ref[1], u_now[...], rec_ref[1])
            q_out[...] = q_diag
            s_out[...] = q_rhs
            give(q_pieces(level), level, stride, whole_q)
            s_copy(level, stride).start()
            r_copy(level, stride).wait_send()
            if not last:
                given(u_pieces(level), level, -stride, split_l)
            given(x_pieces(level), level, -stride, split_l)
            given(q_pieces(level), level, stride, whole_q)
            s_copy(level, stride).wait_send()

        @pl.when(phase == 0)
        def _():
            complete(level, stride, u_now, split_l)
            relay(q_pieces(level), level, whole_q)
            take(q_pieces(level), level, whole_q)
            s_copy(level, stride).wait_recv()
            mirror(q_in.at[level - 1])
            d_now[...] -= q_in[level - 1]
            rec_ref[1] -= s_in[level - 1]
            if not last:
                relayed(u_pieces(level), level, split_l)
            relayed(x_pieces(level), level, split_l)
            relayed(q_pieces(level), level, whole_q)

    @pl.when(lax.rem(me + 1, 2 ** (LEVELS - 1)) == 0)
    def _():
        inv_ref[1] = invert(d_now[...])

    r_copy(0, 1).wait_send()
    given(u_pieces(0), 0, -1, whole_out)
    given(x_pieces(0), 0, -1, whole_out)
    relayed(u_pieces(0), 0, whole_in)
    relayed(x_pieces(0), 0, whole_in)


def body(diag_block, coupling, right_side):
    orbitals, columns = right_side.shape[1:]
    tiles = orbitals // TILE
    square, side = (orbitals, orbitals), (orbitals, columns)
    ways = lax.axis_size("rhs")
    slots = 2 + 2 * tiles + ways
    vmem = pl.BlockSpec(memory_space=pltpu.VMEM)
    return pl.pallas_call(
        functools.partial(kernel, lax.axis_size("layer"), ways),
        out_shape=(
            jax.ShapeDtypeStruct(diag_block.shape, jnp.float32),
            jax.ShapeDtypeStruct(right_side.shape, jnp.float32),
        ),
        in_specs=[vmem] * 3,
        out_specs=(vmem, vmem),
        scratch_shapes=[
            pltpu.VMEM(square, jnp.float32),
            pltpu.VMEM(square, jnp.float32),
            pltpu.VMEM((LEVELS,) + square, jnp.float32),
            pltpu.VMEM((LEVELS - 1,) + square, jnp.float32),
            pltpu.VMEM((LEVELS,) + side, jnp.float32),
            pltpu.VMEM(square, jnp.float32),
            pltpu.VMEM((LEVELS - 1,) + square, jnp.float32),
            pltpu.VMEM(side, jnp.float32),
            pltpu.VMEM((LEVELS - 1,) + side, jnp.float32),
            pltpu.SemaphoreType.DMA((LEVELS, slots)),
            pltpu.SemaphoreType.DMA((LEVELS, slots)),
            pltpu.SemaphoreType.DMA((LEVELS, slots, max(1, ways - 1))),
        ],
        compiler_params=pltpu.CompilerParams(
            collective_id=0, has_side_effects=True, vmem_limit_bytes=48 * 2 ** 20
        ),
    )(diag_block, coupling, right_side)


def solution(mesh):
    return jax.shard_map(
        body,
        mesh=mesh,
        in_specs=(P("layer", None, None), P("layer", None, None), P("layer", None, "rhs")),
        out_specs=(P("layer", None, None), P("layer", None, "rhs")),
        check_vma=False,
    )
```

```python
import functools

import jax
import jax.numpy as jnp
from jax import lax
from jax.experimental import pallas as pl
from jax.experimental.pallas import tpu as pltpu
from jax.sharding import PartitionSpec as P

LEVELS = 3
TILE = 128


def split(value):
    high = value.astype(jnp.bfloat16)
    return high, (value - high.astype(jnp.float32)).astype(jnp.bfloat16)


def matmul(first, second, transposed=False):
    dims = (((1,), (1 if transposed else 0,)), ((), ()))

    def one(a, b):
        return lax.dot_general(a, b, dims, preferred_element_type=jnp.float32)

    return one(first[0], second[0]) + (one(first[0], second[1]) + one(first[1], second[0]))


def beside(first, second):
    return tuple(jnp.concatenate(pair, axis=1) for pair in zip(first, second))


def invert(block):
    orbitals = block.shape[0]
    rows = lax.broadcasted_iota(jnp.int32, (orbitals, orbitals), 0)
    columns = lax.broadcasted_iota(jnp.int32, (orbitals, orbitals), 1)
    on_diag = rows == columns
    trace = jnp.sum(jnp.where(on_diag, block, 0.0), axis=(0, 1), keepdims=True)
    scale = orbitals / trace
    identity = jnp.where(on_diag, 1.0, 0.0)
    err = identity - scale * block
    err_parts = split(err)
    square = matmul(err_parts, err_parts)
    square_parts = split(square)
    both = matmul(square_parts, beside(err_parts, square_parts))
    rest = err + (square + both[:, :orbitals])
    fourth = both[:, orbitals:]
    return scale * (identity + (rest + (fourth + matmul(split(rest), split(fourth)))))


def kernel(size, ways, d_ref, u_ref, r_ref, inv_ref, rec_ref, d_now, u_now, x_in, u_in, r_in,
           q_out, q_in, s_out, s_in, send_sem, recv_sem, pass_sem):
    me = lax.axis_index("layer")
    side = lax.axis_index("rhs")
    orbitals = d_ref.shape[1]
    tiles = orbitals // TILE

    def at(distance):
        return {"layer": lax.rem(me + distance + size, size)}

    def across(hop):
        return {"rhs": lax.rem(side + hop, ways)}

    strides = [2 ** level for level in range(LEVELS - 1)]
    partners = [sign * stride for stride in strides for sign in (1, -1)]
    barrier = pltpu.get_barrier_semaphore()
    for distance in partners:
        pl.semaphore_signal(barrier, inc=1, device_id=at(distance), device_id_type=pl.DeviceIdType.MESH)
    for hop in range(1, ways):
        pl.semaphore_signal(barrier, inc=1, device_id=across(hop), device_id_type=pl.DeviceIdType.MESH)
    pl.semaphore_wait(barrier, len(partners) + ways - 1)

    def remote(src, dst, level, slot, distance):
        return pltpu.make_async_remote_copy(
            src_ref=src, dst_ref=dst, send_sem=send_sem.at[level, slot],
            recv_sem=recv_sem.at[level, slot], device_id=at(distance),
            device_id_type=pl.DeviceIdType.MESH,
        )

    def triangle(src, dst, slot):
        pieces = []
        for i in range(tiles):
            part = (pl.ds(i * TILE, TILE), pl.ds(i * TILE, orbitals - i * TILE))
            pieces.append((src.at[part], dst.at[part], slot + i, min(i, ways - 1)))
        return pieces

    def bands(src, dst, slot):
        rows = orbitals // ways
        parts = [pl.ds(i * rows, rows) for i in range(ways)]
        return [(src.at[part], dst.at[part], slot + i, i) for i, part in enumerate(parts)]

    def u_pieces(level):
        return bands(u_ref.at[0] if level == 0 else u_now, u_in.at[level], 2 + 2 * tiles)

    def x_pieces(level):
        return triangle(inv_ref.at[min(level, 1)], x_in.at[level], 1)

    def q_pieces(level):
        return triangle(q_out, q_in.at[level - 1], 1 + tiles)

    def r_copy(level, stride):
        src = r_ref.at[0] if level == 0 else rec_ref.at[1]
        return remote(src, r_in.at[level], level, 0, -stride)

    def s_copy(level, stride):
        return remote(s_out, s_in.at[level - 1], level, 1 + 2 * tiles, stride)

    def mine(owner, whole):
        return jnp.logical_or(side == owner, whole)

    def give(pieces, level, distance, whole):
        for src, dst, slot, owner in pieces:
            @pl.when(mine(owner, whole))
            def _():
                remote(src, dst, level, slot, distance).start()

    def given(pieces, level, distance, whole):
        for src, dst, slot, owner in pieces:
            @pl.when(mine(owner, whole))
            def _():
                remote(src, dst, level, slot, distance).wait_send()

    def passing(dst, level, slot, hop):
        return pltpu.make_async_remote_copy(
            src_ref=dst, dst_ref=dst, send_sem=pass_sem.at[level, slot, hop - 1],
            recv_sem=recv_sem.at[level, slot], device_id=across(hop),
            device_id_type=pl.DeviceIdType.MESH,
        )

    def relays(owner, whole):
        return jnp.logical_and(side == owner, jnp.logical_not(whole))

    def relay(pieces, level, whole):
        for src, dst, slot, owner in pieces:
            @pl.when(relays(owner, whole))
            def _():
                remote(src, dst, level, slot, 1).wait_recv()
                for hop in range(1, ways):
                    passing(dst, level, slot, hop).start()

    def take(pieces, level, whole):
        for src, dst, slot, owner in pieces:
            @pl.when(jnp.logical_not(relays(owner, whole)))
            def _():
                remote(src, dst, level, slot, 1).wait_recv()

    def relayed(pieces, level, whole):
        for src, dst, slot, owner in pieces:
            @pl.when(relays(owner, whole))
            def _():
                for hop in range(1, ways):
                    passing(dst, level, slot, hop).wait_send()

    def mirror(ref):
        for i in range(tiles):
            for j in range(i + 1, tiles):
                low, high = pl.ds(i * TILE, TILE), pl.ds(j * TILE, TILE)
                ref[high, low] = ref[low, high].T

    def right_part(approx, u_self, r_self):
        parts = split(approx)
        turned = split(u_self.T)
        solved = matmul(parts, beside(split(u_self), split(r_self)))
        reduced = matmul(turned, split(solved))
        return reduced[:, :orbitals], reduced[:, orbitals:]

    def complete(level, stride, u_left, whole):
        last = level == LEVELS - 1
        if not last and level > 0:
            relay(u_pieces(level), level, whole)
        relay(x_pieces(level), level, whole)
        take(x_pieces(level), level, whole)
        mirror(x_in.at[level])
        left = split(u_left[...])
        through = split(matmul(left, split(x_in[level])))
        d_now[...] -= matmul(through, left, transposed=True)
        if not last:
            take(u_pieces(level), level, whole)
        r_copy(level, stride).wait_recv()
        if last:
            rec_ref[1] -= matmul(through, split(r_in[level]))
        else:
            left_part = matmul(through, beside(split(u_in[level]), split(r_in[level])))
            u_now[...] = -left_part[:, :orbitals]
            rec_ref[1] -= left_part[:, orbitals:]

    whole_out = lax.rem(me, 2) == 1
    whole_in = lax.rem(me, 2) == 0
    give(u_pieces(0), 0, -1, whole_out)
    rec_ref[0] = r_ref[0]
    inv_ref[0] = invert(d_ref[0])
    give(x_pieces(0), 0, -1, whole_out)
    r_copy(0, 1).start()
    relay(u_pieces(0), 0, whole_in)
    q_diag, q_rhs = right_part(inv_ref[0], u_ref[0], r_ref[0])
    d_now[...] = d_ref[1] - q_diag
    rec_ref[1] = r_ref[1] - q_rhs
    complete(0, 1, u_ref.at[1], whole_in)

    for level in range(1, LEVELS):
        stride = 2 ** (level - 1)
        phase = lax.rem(me + 1, 2 * stride)
        last = level == LEVELS - 1
        whole_q = lax.rem(me, 1) == (0 if level == 1 else 1)
        split_l = lax.rem(me, 1) == 1

        @pl.when(phase == stride)
        def _():
            if last:
                r_copy(level, stride).start()
            else:
                give(u_pieces(level), level, -stride, split_l)
            inv_ref[1] = invert(d_now[...])
            give(x_pieces(level), level, -stride, split_l)
            if not last:
                r_copy(level, stride).start()
            q_diag, q_rhs = right_part(inv_ref[1], u_now[...], rec_ref[1])
            q_out[...] = q_diag
            s_out[...] = q_rhs
            give(q_pieces(level), level, stride, whole_q)
            s_copy(level, stride).start()
            r_copy(level, stride).wait_send()
            if not last:
                given(u_pieces(level), level, -stride, split_l)
            given(x_pieces(level), level, -stride, split_l)
            given(q_pieces(level), level, stride, whole_q)
            s_copy(level, stride).wait_send()

        @pl.when(phase == 0)
        def _():
            complete(level, stride, u_now, split_l)
            relay(q_pieces(level), level, whole_q)
            take(q_pieces(level), level, whole_q)
            s_copy(level, stride).wait_recv()
            mirror(q_in.at[level - 1])
            d_now[...] -= q_in[level - 1]
            rec_ref[1] -= s_in[level - 1]
            if not last:
                relayed(u_pieces(level), level, split_l)
            relayed(x_pieces(level), level, split_l)
            relayed(q_pieces(level), level, whole_q)

    @pl.when(lax.rem(me + 1, 2 ** (LEVELS - 1)) == 0)
    def _():
        inv_ref[1] = invert(d_now[...])

    r_copy(0, 1).wait_send()
    given(u_pieces(0), 0, -1, whole_out)
    given(x_pieces(0), 0, -1, whole_out)
    relayed(u_pieces(0), 0, whole_in)
    relayed(x_pieces(0), 0, whole_in)


def body(diag_block, coupling, right_side):
    orbitals, columns = right_side.shape[1:]
    tiles = orbitals // TILE
    square, side = (orbitals, orbitals), (orbitals, columns)
    ways = lax.axis_size("rhs")
    slots = 2 + 2 * tiles + ways
    vmem = pl.BlockSpec(memory_space=pltpu.VMEM)
    return pl.pallas_call(
        functools.partial(kernel, lax.axis_size("layer"), ways),
        out_shape=(
            jax.ShapeDtypeStruct(diag_block.shape, jnp.float32),
            jax.ShapeDtypeStruct(right_side.shape, jnp.float32),
        ),
        in_specs=[vmem] * 3,
        out_specs=(vmem, vmem),
        scratch_shapes=[
            pltpu.VMEM(square, jnp.float32),
            pltpu.VMEM(square, jnp.float32),
            pltpu.VMEM((LEVELS,) + square, jnp.float32),
            pltpu.VMEM((LEVELS - 1,) + square, jnp.float32),
            pltpu.VMEM((LEVELS,) + side, jnp.float32),
            pltpu.VMEM(square, jnp.float32),
            pltpu.VMEM((LEVELS - 1,) + square, jnp.float32),
            pltpu.VMEM(side, jnp.float32),
            pltpu.VMEM((LEVELS - 1,) + side, jnp.float32),
            pltpu.SemaphoreType.DMA((LEVELS, slots)),
            pltpu.SemaphoreType.DMA((LEVELS, slots)),
            pltpu.SemaphoreType.DMA((LEVELS, slots, max(1, ways - 1))),
        ],
        compiler_params=pltpu.CompilerParams(
            collective_id=0, has_side_effects=True, vmem_limit_bytes=48 * 2 ** 20
        ),
    )(diag_block, coupling, right_side)


def solution(mesh):
    return jax.shard_map(
        body,
        mesh=mesh,
        in_specs=(P("layer", None, None), P("layer", None, None), P("layer", None, "rhs")),
        out_specs=(P("layer", None, None), P("layer", None, "rhs")),
        check_vma=False,
    )
```

```python
import functools

import jax
import jax.numpy as jnp
from jax import lax
from jax.experimental import pallas as pl
from jax.experimental.pallas import tpu as pltpu
from jax.sharding import PartitionSpec as P

LEVELS = 3
TILE = 128


def split(value):
    high = value.astype(jnp.bfloat16)
    return high, (value - high.astype(jnp.float32)).astype(jnp.bfloat16)


def matmul(first, second, transposed=False):
    dims = (((1,), (1 if transposed else 0,)), ((), ()))

    def one(a, b):
        return lax.dot_general(a, b, dims, preferred_element_type=jnp.float32)

    return one(first[0], second[0]) + (one(first[0], second[1]) + one(first[1], second[0]))


def beside(first, second):
    return tuple(jnp.concatenate(pair, axis=1) for pair in zip(first, second))


def invert(block):
    orbitals = block.shape[0]
    rows = lax.broadcasted_iota(jnp.int32, (orbitals, orbitals), 0)
    columns = lax.broadcasted_iota(jnp.int32, (orbitals, orbitals), 1)
    on_diag = rows == columns
    trace = jnp.sum(jnp.where(on_diag, block, 0.0), axis=(0, 1), keepdims=True)
    scale = orbitals / trace
    identity = jnp.where(on_diag, 1.0, 0.0)
    err = identity - scale * block
    err_parts = split(err)
    square = matmul(err_parts, err_parts)
    square_parts = split(square)
    both = matmul(square_parts, beside(err_parts, square_parts))
    rest = err + (square + both[:, :orbitals])
    fourth = both[:, orbitals:]
    return scale * (identity + (rest + (fourth + matmul(split(rest), split(fourth)))))


def kernel(size, ways, d_ref, u_ref, r_ref, inv_ref, rec_ref, d_now, u_now, x_in, u_in, r_in,
           q_out, q_in, s_out, s_in, send_sem, recv_sem, pass_sem):
    me = lax.axis_index("layer")
    side = lax.axis_index("rhs")
    orbitals = d_ref.shape[1]
    tiles = orbitals // TILE

    def at(distance):
        return {"layer": lax.rem(me + distance + size, size)}

    def across(hop):
        return {"rhs": lax.rem(side + hop, ways)}

    strides = [2 ** level for level in range(LEVELS - 1)]
    partners = [sign * stride for stride in strides for sign in (1, -1)]
    barrier = pltpu.get_barrier_semaphore()
    for distance in partners:
        pl.semaphore_signal(barrier, inc=1, device_id=at(distance), device_id_type=pl.DeviceIdType.MESH)
    for hop in range(1, ways):
        pl.semaphore_signal(barrier, inc=1, device_id=across(hop), device_id_type=pl.DeviceIdType.MESH)
    pl.semaphore_wait(barrier, len(partners) + ways - 1)

    def remote(src, dst, level, slot, distance):
        return pltpu.make_async_remote_copy(
            src_ref=src, dst_ref=dst, send_sem=send_sem.at[level, slot],
            recv_sem=recv_sem.at[level, slot], device_id=at(distance),
            device_id_type=pl.DeviceIdType.MESH,
        )

    def triangle(src, dst, slot):
        pieces = []
        for i in range(tiles):
            part = (pl.ds(i * TILE, TILE), pl.ds(i * TILE, orbitals - i * TILE))
            pieces.append((src.at[part], dst.at[part], slot + i, min(i, ways - 1)))
        return pieces

    def bands(src, dst, slot):
        rows = orbitals // ways
        parts = [pl.ds(i * rows, rows) for i in range(ways)]
        return [(src.at[part], dst.at[part], slot + i, i) for i, part in enumerate(parts)]

    def u_pieces(level):
        return bands(u_ref.at[0] if level == 0 else u_now, u_in.at[level], 2 + 2 * tiles)

    def x_pieces(level):
        return triangle(inv_ref.at[min(level, 1)], x_in.at[level], 1)

    def q_pieces(level):
        return triangle(q_out, q_in.at[level - 1], 1 + tiles)

    def r_copy(level, stride):
        src = r_ref.at[0] if level == 0 else rec_ref.at[1]
        return remote(src, r_in.at[level], level, 0, -stride)

    def s_copy(level, stride):
        return remote(s_out, s_in.at[level - 1], level, 1 + 2 * tiles, stride)

    def mine(owner, whole):
        return jnp.logical_or(side == owner, whole)

    def give(pieces, level, distance, whole):
        for src, dst, slot, owner in pieces:
            @pl.when(mine(owner, whole))
            def _():
                remote(src, dst, level, slot, distance).start()

    def given(pieces, level, distance, whole):
        for src, dst, slot, owner in pieces:
            @pl.when(mine(owner, whole))
            def _():
                remote(src, dst, level, slot, distance).wait_send()

    def passing(dst, level, slot, hop):
        return pltpu.make_async_remote_copy(
            src_ref=dst, dst_ref=dst, send_sem=pass_sem.at[level, slot, hop - 1],
            recv_sem=recv_sem.at[level, slot], device_id=across(hop),
            device_id_type=pl.DeviceIdType.MESH,
        )

    def relays(owner, whole):
        return jnp.logical_and(side == owner, jnp.logical_not(whole))

    def relay(pieces, level, whole):
        for src, dst, slot, owner in pieces:
            @pl.when(relays(owner, whole))
            def _():
                remote(src, dst, level, slot, 1).wait_recv()
                for hop in range(1, ways):
                    passing(dst, level, slot, hop).start()

    def take(pieces, level, whole):
        for src, dst, slot, owner in pieces:
            @pl.when(jnp.logical_not(relays(owner, whole)))
            def _():
                remote(src, dst, level, slot, 1).wait_recv()

    def relayed(pieces, level, whole):
        for src, dst, slot, owner in pieces:
            @pl.when(relays(owner, whole))
            def _():
                for hop in range(1, ways):
                    passing(dst, level, slot, hop).wait_send()

    def mirror(ref):
        for i in range(tiles):
            for j in range(i + 1, tiles):
                low, high = pl.ds(i * TILE, TILE), pl.ds(j * TILE, TILE)
                ref[high, low] = ref[low, high].T

    def right_part(approx, u_self, r_self):
        parts = split(approx)
        turned = split(u_self.T)
        solved = matmul(parts, beside(split(u_self), split(r_self)))
        reduced = matmul(turned, split(solved))
        return reduced[:, :orbitals], reduced[:, orbitals:]

    def complete(level, stride, u_left, whole):
        last = level == LEVELS - 1
        if not last and level > 0:
            relay(u_pieces(level), level, whole)
        relay(x_pieces(level), level, whole)
        take(x_pieces(level), level, whole)
        mirror(x_in.at[level])
        left = split(u_left[...])
        through = split(matmul(left, split(x_in[level])))
        d_now[...] -= matmul(through, left, transposed=True)
        if not last:
            take(u_pieces(level), level, whole)
        r_copy(level, stride).wait_recv()
        if last:
            rec_ref[1] -= matmul(through, split(r_in[level]))
        else:
            left_part = matmul(through, beside(split(u_in[level]), split(r_in[level])))
            u_now[...] = -left_part[:, :orbitals]
            rec_ref[1] -= left_part[:, orbitals:]

    whole_out = lax.rem(me, 2) == 1
    whole_in = lax.rem(me, 2) == 0
    give(u_pieces(0), 0, -1, whole_out)
    rec_ref[0] = r_ref[0]
    inv_ref[0] = invert(d_ref[0])
    give(x_pieces(0), 0, -1, whole_out)
    r_copy(0, 1).start()
    relay(u_pieces(0), 0, whole_in)
    q_diag, q_rhs = right_part(inv_ref[0], u_ref[0], r_ref[0])
    d_now[...] = d_ref[1] - q_diag
    rec_ref[1] = r_ref[1] - q_rhs
    complete(0, 1, u_ref.at[1], whole_in)

    for level in range(1, LEVELS):
        stride = 2 ** (level - 1)
        phase = lax.rem(me + 1, 2 * stride)
        last = level == LEVELS - 1
        whole_q = lax.rem(me, 1) == 0
        split_l = lax.rem(me, 1) == 1

        @pl.when(phase == stride)
        def _():
            if last:
                r_copy(level, stride).start()
            else:
                give(u_pieces(level), level, -stride, split_l)
            inv_ref[1] = invert(d_now[...])
            give(x_pieces(level), level, -stride, split_l)
            if not last:
                r_copy(level, stride).start()
            q_diag, q_rhs = right_part(inv_ref[1], u_now[...], rec_ref[1])
            q_out[...] = q_diag
            s_out[...] = q_rhs
            give(q_pieces(level), level, stride, whole_q)
            s_copy(level, stride).start()
            r_copy(level, stride).wait_send()
            if not last:
                given(u_pieces(level), level, -stride, split_l)
            given(x_pieces(level), level, -stride, split_l)
            given(q_pieces(level), level, stride, whole_q)
            s_copy(level, stride).wait_send()

        @pl.when(phase == 0)
        def _():
            complete(level, stride, u_now, split_l)
            relay(q_pieces(level), level, whole_q)
            take(q_pieces(level), level, whole_q)
            s_copy(level, stride).wait_recv()
            mirror(q_in.at[level - 1])
            d_now[...] -= q_in[level - 1]
            rec_ref[1] -= s_in[level - 1]
            if not last:
                relayed(u_pieces(level), level, split_l)
            relayed(x_pieces(level), level, split_l)
            relayed(q_pieces(level), level, whole_q)

    @pl.when(lax.rem(me + 1, 2 ** (LEVELS - 1)) == 0)
    def _():
        inv_ref[1] = invert(d_now[...])

    r_copy(0, 1).wait_send()
    given(u_pieces(0), 0, -1, whole_out)
    given(x_pieces(0), 0, -1, whole_out)
    relayed(u_pieces(0), 0, whole_in)
    relayed(x_pieces(0), 0, whole_in)


def body(diag_block, coupling, right_side):
    orbitals, columns = right_side.shape[1:]
    tiles = orbitals // TILE
    square, side = (orbitals, orbitals), (orbitals, columns)
    ways = lax.axis_size("rhs")
    slots = 2 + 2 * tiles + ways
    vmem = pl.BlockSpec(memory_space=pltpu.VMEM)
    return pl.pallas_call(
        functools.partial(kernel, lax.axis_size("layer"), ways),
        out_shape=(
            jax.ShapeDtypeStruct(diag_block.shape, jnp.float32),
            jax.ShapeDtypeStruct(right_side.shape, jnp.float32),
        ),
        in_specs=[vmem] * 3,
        out_specs=(vmem, vmem),
        scratch_shapes=[
            pltpu.VMEM(square, jnp.float32),
            pltpu.VMEM(square, jnp.float32),
            pltpu.VMEM((LEVELS,) + square, jnp.float32),
            pltpu.VMEM((LEVELS - 1,) + square, jnp.float32),
            pltpu.VMEM((LEVELS,) + side, jnp.float32),
            pltpu.VMEM(square, jnp.float32),
            pltpu.VMEM((LEVELS - 1,) + square, jnp.float32),
            pltpu.VMEM(side, jnp.float32),
            pltpu.VMEM((LEVELS - 1,) + side, jnp.float32),
            pltpu.SemaphoreType.DMA((LEVELS, slots)),
            pltpu.SemaphoreType.DMA((LEVELS, slots)),
            pltpu.SemaphoreType.DMA((LEVELS, slots, max(1, ways - 1))),
        ],
        compiler_params=pltpu.CompilerParams(
            collective_id=0, has_side_effects=True, vmem_limit_bytes=48 * 2 ** 20
        ),
    )(diag_block, coupling, right_side)


def solution(mesh):
    return jax.shard_map(
        body,
        mesh=mesh,
        in_specs=(P("layer", None, None), P("layer", None, None), P("layer", None, "rhs")),
        out_specs=(P("layer", None, None), P("layer", None, "rhs")),
        check_vma=False,
    )
```
